32 devices in a mesh: pair: 4 (over z), blk: 8 (over y, x, core).
Axes of the slice: x: 2, y: 2, z: 4, core: 2. Of those that a mesh axis runs over, the one named last changes fastest.
Arguments:
- spectra: bfloat16 [3000, 4096], P(None, ('pair', 'blk')), may hold values from -24 to 24
- wedge_ids: int32 [2048], P(('pair', 'blk')), may hold values from 0 to 7
- tilt_limits: int32 [8, 2], replicated, may hold values from 4 to 15
- term_freqs: int32 [3, 3000], replicated, may hold values from -12 to 11, as said below
Outputs:
- best_match: float32 [2048, 256], P(('pair', 'blk'))
The draws below stay inside these ranges and needn't reach their ends.
Inputs may be any that keep to these rules, and one draw needn't show every extreme that they name: `term_freqs`: each entry is a frequency index along one axis of the 24-cell box.
All inputs are finite; a program needn't handle non-finite values.
Results may differ from the reference program's by a relative error of at most 0.00065.
Values may be sent and summed in bfloat16 or wider, within the bound.
No kernel may reach another device: no remote copies, remote signals or barrier semaphores. Data moves between devices by JAX's collectives and lax.ppermute only.
A program may use at most 64 MiB of HBM per device.

```python
import math
import jax
import jax.numpy as jnp
from jax import lax

TERMS = 3000
BOX = 24
CLASSES = 8
RADIUS = 1
SHIFTS = 27
PART_DEV = 64
STEPS = 2
ROUND = 2
PARTICLES = 2048
N_PAIR = 4
N_BLK = 8


def term_grid(key):
    return jax.random.randint(jax.random.fold_in(key, 101), (3, TERMS), -(BOX // 2), BOX // 2, dtype=jnp.int32)


def loguniform(key, shape, lower, upper):
    return jnp.exp(jax.random.uniform(key, shape, jnp.float32, math.log(lower), math.log(upper)))


def draw_term_freqs(key, part):
    frequency_grid = term_grid(key)
    return frequency_grid


def draw_spectra(key, part):
    frequency_grid = term_grid(key)
    key = jax.random.fold_in(key, 7)
    subkeys = jax.random.split(key, 5)
    noise_part = jax.random.normal(subkeys[0], (2, TERMS, PARTICLES), jnp.float32)
    amplitude = loguniform(subkeys[1], (PARTICLES,), 0.15, 1.5)
    term_scale = loguniform(subkeys[2], (TERMS,), 0.3, 3.0)
    signal = jax.random.normal(subkeys[3], (2, TERMS), jnp.float32)
    true_offsets = jax.random.randint(subkeys[4], (3, PARTICLES), -1, 2, dtype=jnp.int32)
    phase_turns = frequency_grid[0][:, None] * true_offsets[0][None, :] + frequency_grid[1][:, None] * true_offsets[1][None, :] + frequency_grid[2][:, None] * true_offsets[2][None, :]
    phase_angle = phase_turns.astype(jnp.float32) * (2.0 * math.pi / BOX)
    cosine_part = jnp.cos(phase_angle)
    sine_part = jnp.sin(phase_angle)
    real_part = signal[0][:, None] * cosine_part + signal[1][:, None] * sine_part
    imag_part = signal[1][:, None] * cosine_part - signal[0][:, None] * sine_part
    spectra_value = term_scale[None, :, None] * (amplitude[None, None, :] * jnp.stack([real_part, imag_part]) + noise_part)
    spectra_value = jnp.clip(spectra_value, -24.0, 24.0)
    packed = spectra_value.reshape(2, TERMS, PARTICLES // PART_DEV, PART_DEV)
    packed = jnp.transpose(packed, (1, 2, 0, 3)).reshape(TERMS, 2 * PARTICLES)
    return packed.astype(jnp.bfloat16)


def place_ends(array, stream_key, smallest, top_value):
    longest = array.shape.index(max(array.shape))
    spots = []
    for shift in (0, 1):
        where = [jax.random.randint(jax.random.fold_in(stream_key, axis), (), 0, length) for axis, length in enumerate(array.shape)]
        where[longest] = (where[longest] + shift) % array.shape[longest]
        spots.append(tuple(where))
    return array.at[spots[0]].set(smallest).at[spots[1]].set(top_value)


def setup_inputs(seed: int = 0) -> dict:
    arg_keys = jax.random.split(jax.random.key(seed), 5)
    return {
        "spectra": draw_spectra(jax.random.fold_in(arg_keys[4], 71), 0),
        "wedge_ids": place_ends(jax.random.randint(arg_keys[1], (PARTICLES,), 0, CLASSES), jax.random.fold_in(arg_keys[1], 1), 0, CLASSES - 1).astype(jnp.int32),
        "tilt_limits": place_ends(jax.random.randint(arg_keys[2], (CLASSES, 2), 4, 16), jax.random.fold_in(arg_keys[2], 1), 4, 15).astype(jnp.int32),
        "term_freqs": draw_term_freqs(jax.random.fold_in(arg_keys[4], 71), 0),
    }


epsilon = 1e-06

def wedge_table(term_freqs, tilt_limits):
    first_axis = term_freqs[0][:, None]
    third_axis = term_freqs[2][:, None]
    limit_value = jnp.where(first_axis * third_axis >= 0, tilt_limits[:, 0][None, :], tilt_limits[:, 1][None, :])
    measured = 4 * third_axis * third_axis <= limit_value * first_axis * first_axis
    return jnp.where(measured, 1.0, 0.0).astype(jnp.float32)

def shift_phases(term_freqs):
    span_cells = 2 * RADIUS + 1
    shift_index = jnp.arange(SHIFTS, dtype=jnp.int32)
    offset_first = shift_index // (span_cells * span_cells) - RADIUS
    offset_second = shift_index // span_cells % span_cells - RADIUS
    offset_third = shift_index % span_cells - RADIUS
    phase_turns = offset_first[:, None] * term_freqs[0][None, :] + offset_second[:, None] * term_freqs[1][None, :] + offset_third[:, None] * term_freqs[2][None, :]
    phase_angle = phase_turns.astype(jnp.float32) * (2.0 * math.pi / BOX)
    return (jnp.cos(phase_angle), jnp.sin(phase_angle))

def block_data(spectra, wedge_ids, table, block_index):
    row_start = (block_index * PART_DEV).astype(jnp.int32)
    particle_block = lax.dynamic_slice_in_dim(spectra, row_start, PART_DEV, 2)
    block_ids = lax.dynamic_slice_in_dim(wedge_ids, row_start, PART_DEV, 0)
    measured = jnp.take(table, block_ids, axis=1)
    masked = particle_block * measured.astype(jnp.bfloat16)[None]
    power_terms = lax.optimization_barrier(jnp.sum(jnp.square(masked.astype(jnp.float32)), axis=0))
    class_power = jnp.dot(power_terms.T, table, precision=lax.Precision.HIGHEST, preferred_element_type=jnp.float32)
    return (masked, block_ids, class_power)

def reference(spectra, wedge_ids, tilt_limits, term_freqs):
    unpacked = spectra.reshape(TERMS, PARTICLES // PART_DEV, 2, PART_DEV)
    unpacked = jnp.transpose(unpacked, (2, 0, 1, 3)).reshape(2, TERMS, PARTICLES)
    table = wedge_table(term_freqs, tilt_limits)
    cosine_table, sine_table = shift_phases(term_freqs)
    offset_list = [offset for offset in range(1, STEPS + 1)] + [-offset for offset in range(1, STEPS + 1)]

    def one_block(block_index):
        group_index = block_index // N_BLK
        place_index = block_index % N_BLK
        partner = jnp.bitwise_xor(group_index, ROUND)
        row_block, row_ids, row_power = block_data(unpacked, wedge_ids, table, block_index)
        fetched = [block_data(unpacked, wedge_ids, table, partner * N_BLK + (place_index + offset) % N_BLK) for offset in offset_list]
        column_block = jnp.concatenate([entry[0] for entry in fetched], axis=2).astype(jnp.float32)
        column_ids = jnp.concatenate([entry[1] for entry in fetched], axis=0)
        column_power = jnp.concatenate([entry[2] for entry in fetched], axis=0)
        real_part = row_block[0].astype(jnp.float32)
        imag_part = row_block[1].astype(jnp.float32)

        def one_turn(running, shift_index):
            cosine_row = cosine_table[shift_index][:, None]
            sine_row = sine_table[shift_index][:, None]
            rotated = jnp.stack([real_part * cosine_row + imag_part * sine_row, imag_part * cosine_row - real_part * sine_row])
            scores = jnp.einsum('akp,akq->pq', rotated, column_block, precision=lax.Precision.HIGHEST)
            return (jnp.maximum(running, scores), None)
        starting = jnp.full((PART_DEV, 2 * STEPS * PART_DEV), -jnp.inf, jnp.float32)
        largest, _ = lax.scan(one_turn, starting, jnp.arange(SHIFTS, dtype=jnp.int32))
        row_norm = jnp.take(row_power, column_ids, axis=1)
        column_norm = jnp.take(column_power, row_ids, axis=1).T
        return largest * lax.rsqrt(row_norm * column_norm + epsilon)
    blocks = lax.map(one_block, jnp.arange(N_PAIR * N_BLK, dtype=jnp.int32))
    return blocks.reshape(PARTICLES, 2 * STEPS * PART_DEV)
```

```python
import math

import jax
import jax.numpy as jnp
from jax import lax
from jax.experimental import pallas as pl
from jax.experimental.pallas import tpu as pltpu
from jax.sharding import PartitionSpec as P

BOX = 24
RADIUS = 1
ROUND = 2
EPSILON = 1e-06
PAYLOAD = 32
LANES = 128
CUTS = (1024, 1024, 1024)
AXES = ("pair", "blk")
F32 = jnp.float32
BF16 = jnp.bfloat16

SHIFTS = tuple(
    (a, b, c)
    for a in range(-RADIUS, RADIUS + 1)
    for b in range(-RADIUS, RADIUS + 1)
    for c in range(-RADIUS, RADIUS + 1)
    if (a, b, c) > (0, 0, 0)
)
COUNT = len(SHIFTS)
VMEM = pl.BlockSpec(memory_space=pltpu.VMEM)
SMEM = pl.BlockSpec(memory_space=pltpu.SMEM)


def near_group(group):
    return (group >> 1 ^ group) & 1 == 0


def permute(value, route):
    pairs_n, blocks_n = lax.axis_size("pair"), lax.axis_size("blk")
    table = []
    for group in range(pairs_n):
        for block in range(blocks_n):
            place = route(group, block, blocks_n)
            if place is not None:
                source = place[0] * blocks_n + place[1] % blocks_n
                table.append((source, group * blocks_n + block))
    return lax.ppermute(value, AXES, table)


def cross_source(group, block, count):
    if near_group(group):
        return None
    return group ^ 1 ^ ROUND, block - 2 if block % 2 == 0 else block


def swap_source(group, block, count):
    if near_group(group):
        return group ^ 1, block + 4 if block % 2 == 0 else block - 2
    return group ^ 1, block if block % 2 == 0 else block - 2


def core_source(group, block, count):
    return group, block ^ 1


def own_back_source(group, block, count):
    if near_group(group):
        return None
    return group ^ 1 ^ ROUND, block + 2 if block % 2 == 0 else block


def first_back_source(group, block, count):
    if near_group(group):
        return group ^ 1, block if block % 2 == 0 else block + 2
    return group ^ ROUND, block - 2 if block % 2 == 0 else block + 2


def second_back_source(group, block, count):
    if near_group(group):
        return group ^ 1, block + 1
    return group ^ ROUND, block - 1 if block % 2 == 0 else block + 1


def wedge_rows(freqs, limits_ref):
    classes = limits_ref.shape[1]
    row = lax.broadcasted_iota(jnp.int32, (classes, 1), 0)
    same_side = jnp.zeros((classes, 1), jnp.int32)
    other_side = jnp.zeros((classes, 1), jnp.int32)
    for index in range(classes):
        same_side = jnp.where(row == index, limits_ref[0, index], same_side)
        other_side = jnp.where(row == index, limits_ref[1, index], other_side)
    first_axis, third_axis = freqs[0:1], freqs[2:3]
    limit = jnp.where(first_axis * third_axis >= 0, same_side, other_side)
    measured = 4 * third_axis * third_axis <= limit * (first_axis * first_axis)
    return jnp.where(measured, 1.0, 0.0).astype(F32)


def chosen_classes(ids_ref, classes):
    ids = ids_ref[...]
    both = jnp.concatenate([ids, ids], axis=1)
    row = lax.broadcasted_iota(jnp.int32, (classes, both.shape[1]), 0)
    return jnp.where(row == both, 1.0, 0.0).astype(F32), both


def mask_rows(spectra, table, chosen):
    measured = jnp.dot(
        table.T.astype(BF16), chosen.astype(BF16), preferred_element_type=F32
    )
    return spectra * measured


def first_mask_kernel(spectra_ref, ids_ref, limits_ref, freqs_ref, out_ref):
    rows = out_ref.shape[0]
    table = wedge_rows(freqs_ref[:, :rows], limits_ref)
    chosen, _ = chosen_classes(ids_ref, limits_ref.shape[1])
    out_ref[...] = mask_rows(spectra_ref[...].astype(F32), table, chosen).astype(BF16)


def split_three(value):
    high = value.astype(BF16).astype(F32)
    rest = value - high
    middle = rest.astype(BF16).astype(F32)
    return high, middle, rest - middle


def rest_mask_kernel(terms, starts, spectra_ref, ids_ref, limits_ref, freqs_ref, *out_refs):
    classes = limits_ref.shape[1]
    half = spectra_ref.shape[1] // 2
    table = wedge_rows(freqs_ref[...], limits_ref)
    chosen, both = chosen_classes(ids_ref, classes)
    spectra = spectra_ref[...].astype(F32)
    power = jnp.zeros((classes, half), F32)
    for index, start in enumerate(starts):
        rows = CUTS[index]
        used = min(rows, terms - start)
        part = spectra[start : start + used]
        if used < rows:
            part = jnp.concatenate([part, jnp.zeros((rows - used, 2 * half), F32)], axis=0)
        masked = mask_rows(part, table[:, start : start + rows], chosen)
        squared = masked * masked
        total = squared + pltpu.roll(squared, half, 1)
        table_part = table[:, start : start + rows].astype(BF16)
        for piece in split_three(total):
            power = power + jnp.dot(
                table_part, piece.astype(BF16), preferred_element_type=F32
            )[:, :half]
        if index == len(starts) - 1:
            pieces = [
                jnp.concatenate([piece, piece], axis=1) for piece in split_three(power)
            ]
            ids = jnp.broadcast_to(both.astype(F32), (classes, 2 * half))
            spare = jnp.zeros((rows - used - PAYLOAD, 2 * half), F32)
            masked = jnp.concatenate([masked[:used], *pieces, ids, spare], axis=0)
        if index > 0:
            out_refs[index - 1][...] = masked.astype(BF16)


def chunk_kernel(used, first, last, near_ref, kept_ref, crossed_ref, got_ref, core_ref,
                 trig_ref, *refs):
    if first:
        total_ref = None
    else:
        total_ref, *refs = refs
    outs, (high_ref, low_ref, other_ref) = refs[:-3], refs[-3:]
    rows, lanes = kept_ref.shape
    half = lanes // 2
    near = near_ref[0] == 1
    own = jnp.where(near, kept_ref[...].astype(F32), crossed_ref[...].astype(F32))
    got = got_ref[...].astype(F32)
    core = core_ref[...].astype(F32)
    other_ref[0:rows, :] = jnp.concatenate([got[:, :half], core[:, :half]], axis=1).astype(BF16)
    other_ref[rows:, :] = jnp.concatenate([got[:, half:], core[:, half:]], axis=1).astype(BF16)
    turned = own.T
    if used < rows:
        lane = lax.broadcasted_iota(jnp.int32, (1, rows), 1)
        turned = jnp.where(lane < used, turned, 0.0)
    real, imag = turned[:half], turned[half:]

    def put(row, part, value):
        high = value.astype(BF16)
        high_ref[row : row + half, part * rows : (part + 1) * rows] = high
        low_ref[row : row + half, part * rows : (part + 1) * rows] = (
            value - high.astype(F32)
        ).astype(BF16)

    plain = 2 * COUNT * half
    high_ref[plain:, 0:rows] = real.astype(BF16)
    high_ref[plain:, rows:] = imag.astype(BF16)
    for index in range(COUNT):
        cosine = trig_ref[index : index + 1, :]
        sine = trig_ref[COUNT + index : COUNT + index + 1, :]
        put(index * half, 0, cosine * real)
        put(index * half, 1, cosine * imag)
        put((COUNT + index) * half, 0, sine * imag)
        put((COUNT + index) * half, 1, -sine * real)
    scores_ref = outs[0]
    scores = jnp.dot(high_ref[...], other_ref[...], preferred_element_type=F32)
    if first:
        scores_ref[...] = scores
    else:
        scores_ref[...] = total_ref[...] + scores
    scores_ref[0:plain] += jnp.dot(low_ref[...], other_ref[...], preferred_element_type=F32)
    if not last:
        return

    largest = scores_ref[plain:]
    for index in range(COUNT):
        even = scores_ref[index * half : (index + 1) * half]
        odd = scores_ref[(COUNT + index) * half : (COUNT + index + 1) * half]
        largest = jnp.maximum(largest, even + jnp.abs(odd))
    classes = PAYLOAD // 4
    extra = slice(used, used + PAYLOAD)
    own_extra = own[extra][:, :half]
    other_extra = jnp.concatenate([got[extra][:, :half], core[extra][:, :half]], axis=1)

    def chosen(ids):
        row = lax.broadcasted_iota(jnp.int32, ids.shape, 0).astype(F32)
        once = jnp.where(row == ids, 1.0, 0.0).astype(F32)
        return jnp.concatenate([once] * 3, axis=0)

    own_chosen = chosen(own_extra[3 * classes :])
    other_chosen = chosen(other_extra[3 * classes :])
    row_norm = jnp.dot(
        own_extra[: 3 * classes].T.astype(BF16),
        other_chosen.astype(BF16),
        preferred_element_type=F32,
    )
    column_norm = jnp.dot(
        own_chosen.T.astype(BF16),
        other_extra[: 3 * classes].astype(BF16),
        preferred_element_type=F32,
    )
    best = largest * lax.rsqrt(row_norm * column_norm + EPSILON)
    outs[1][...] = best
    across = best.T
    outs[2][...] = across[:half]
    outs[3][...] = across[half:]


def chunk_scores(used, first, last, half, near, kept, crossed, got, core, trig, total):
    rows = kept.shape[0]
    score_rows = (2 * COUNT + 1) * half
    out_shape = [jax.ShapeDtypeStruct((score_rows, 2 * half), F32)]
    if last:
        out_shape += [
            jax.ShapeDtypeStruct((half, 2 * half), F32),
            jax.ShapeDtypeStruct((half, half), F32),
            jax.ShapeDtypeStruct((half, half), F32),
        ]
    operands = [near, kept, crossed, got, core, trig] + ([] if first else [total])
    return pl.pallas_call(
        lambda *refs: chunk_kernel(used, first, last, *refs),
        out_shape=out_shape,
        in_specs=[SMEM] + [VMEM] * (len(operands) - 1),
        out_specs=[VMEM] * len(out_shape),
        scratch_shapes=[
            pltpu.VMEM((score_rows, 2 * rows), BF16),
            pltpu.VMEM((score_rows - half, 2 * rows), BF16),
            pltpu.VMEM((2 * rows, 2 * half), BF16),
        ],
        compiler_params=pltpu.CompilerParams(vmem_limit_bytes=28 << 20),
        cost_estimate=pl.CostEstimate(
            flops=4 * score_rows * 2 * rows * 2 * half, bytes_accessed=4 << 20, transcendentals=0
        ),
    )(*operands)


def shards(spectra, wedge_ids, tilt_limits, term_freqs):
    terms, lanes = spectra.shape
    half = lanes // 2
    padded = sum(CUTS)
    starts = [sum(CUTS[:index]) for index in range(len(CUTS))]
    group, block = lax.axis_index("pair"), lax.axis_index("blk")
    near = near_group(group)
    near_flag = near.astype(jnp.int32)[None]
    ids = wedge_ids[None]
    limits = tilt_limits.T

    first_chunk = pl.pallas_call(
        first_mask_kernel,
        grid=(1,),
        out_shape=jax.ShapeDtypeStruct((CUTS[0], lanes), BF16),
        in_specs=[pl.BlockSpec((CUTS[0], lanes), lambda i: (0, 0)), VMEM, SMEM, VMEM],
        out_specs=VMEM,
    )(spectra, ids, limits, term_freqs)
    freqs = jnp.pad(term_freqs, ((0, 0), (0, padded - terms)))
    rest = pl.pallas_call(
        lambda *refs: rest_mask_kernel(terms, starts, *refs),
        out_shape=[jax.ShapeDtypeStruct((rows, lanes), BF16) for rows in CUTS[1:]],
        in_specs=[VMEM, VMEM, SMEM, VMEM],
        out_specs=[VMEM] * (len(CUTS) - 1),
    )(spectra, ids, limits, freqs)
    kept = [first_chunk, *rest]

    shift = jnp.array(SHIFTS, jnp.int32)
    turns = (
        shift[:, 0:1] * freqs[0:1] + shift[:, 1:2] * freqs[1:2] + shift[:, 2:3] * freqs[2:3]
    )
    angle = turns.astype(F32) * (2.0 * math.pi / BOX)
    trig = jnp.concatenate([jnp.cos(angle), jnp.sin(angle)], axis=0)

    crossed = [permute(chunk, cross_source) for chunk in kept]
    got, core = [], []
    for own, far in zip(kept, crossed):
        got.append(permute(jnp.where(near, own, far), swap_source))
        core.append(permute(got[-1], core_source))

    total = None
    for index, start in enumerate(starts):
        used = min(CUTS[index], terms - start)
        total, *tiles = chunk_scores(
            used, index == 0, index == len(starts) - 1, half, near_flag, kept[index],
            crossed[index], got[index], core[index], trig[:, start : start + CUTS[index]], total,
        )
    local, first_tile, second_tile = tiles
    returned = permute(local, own_back_source)
    first_back = permute(first_tile, first_back_source)
    second_back = permute(second_tile, second_back_source)

    mine = jnp.where(near, local, returned)
    got_tile, core_tile = mine[:, :half], mine[:, half:]
    even = block % 2 == 0
    lead = near == even
    return jnp.concatenate(
        [
            jnp.where(lead, second_back, core_tile),
            jnp.where(even, got_tile, first_back),
            jnp.where(lead, core_tile, second_back),
            jnp.where(even, first_back, got_tile),
        ],
        axis=1,
    )


def solution(mesh):
    placed = (P(None, AXES), P(AXES), P(), P())
    return jax.shard_map(
        shards, mesh=mesh, in_specs=placed, out_specs=P(AXES, None), check_vma=False
    )
```

```python
import functools
import math

import jax
import jax.numpy as jnp
from jax import lax
from jax.experimental import pallas as pl
from jax.experimental.pallas import tpu as pltpu
from jax.sharding import PartitionSpec as P

BOX = 24
RADIUS = 1
ROUND = 2
EPSILON = 1e-06
PAYLOAD = 32
LANES = 128
CUTS = (1024, 1024, 1024)
AXES = ("pair", "blk")
F32 = jnp.float32
BF16 = jnp.bfloat16

SHIFTS = tuple(
    (a, b, c)
    for a in range(-RADIUS, RADIUS + 1)
    for b in range(-RADIUS, RADIUS + 1)
    for c in range(-RADIUS, RADIUS + 1)
    if (a, b, c) > (0, 0, 0)
)
COUNT = len(SHIFTS)
SHIFT_ROWS = 16
VMEM = pl.BlockSpec(memory_space=pltpu.VMEM)
SMEM = pl.BlockSpec(memory_space=pltpu.SMEM)
ANY = pl.BlockSpec(memory_space=pl.ANY)
LOW_COST = pl.CostEstimate(flops=1, bytes_accessed=1, transcendentals=0)


def near_group(group):
    return (group >> 1 ^ group) & 1 == 0


def permute(value, route):
    pairs_n, blocks_n = lax.axis_size("pair"), lax.axis_size("blk")
    table = []
    for group in range(pairs_n):
        for block in range(blocks_n):
            place = route(group, block, blocks_n)
            if place is not None:
                source = place[0] * blocks_n + place[1] % blocks_n
                table.append((source, group * blocks_n + block))
    return lax.ppermute(value, AXES, table)


def cross_source(group, block, count):
    if near_group(group):
        return None
    return group ^ 1 ^ ROUND, block - 2 if block % 2 == 0 else block


def swap_source(group, block, count):
    if near_group(group):
        return group ^ 1, block + 4 if block % 2 == 0 else block - 2
    return group ^ 1, block if block % 2 == 0 else block - 2


def core_source(group, block, count):
    return group, block ^ 1


def own_back_source(group, block, count):
    if near_group(group):
        return None
    return group ^ 1 ^ ROUND, block + 2 if block % 2 == 0 else block


def first_back_source(group, block, count):
    if near_group(group):
        return group ^ 1, block if block % 2 == 0 else block + 2
    return group ^ ROUND, block - 2 if block % 2 == 0 else block + 2


def second_back_source(group, block, count):
    if near_group(group):
        return group, block ^ 1
    return group ^ 1 ^ ROUND, block + 3 if block % 2 == 0 else block - 1


def chunk_freqs(freqs_ref, start, rows):
    axes, terms = freqs_ref.shape
    if start + rows <= terms:
        return freqs_ref[:, start : start + rows]
    spare = jnp.zeros((axes, start + rows - terms), jnp.int32)
    return jnp.concatenate([freqs_ref[:, start:], spare], axis=1)


def wedge_rows(freqs, limits_ref):
    classes = limits_ref.shape[1]
    row = lax.broadcasted_iota(jnp.int32, (classes, 1), 0)
    same_side = jnp.zeros((classes, 1), jnp.int32)
    other_side = jnp.zeros((classes, 1), jnp.int32)
    for index in range(classes):
        same_side = jnp.where(row == index, limits_ref[0, index], same_side)
        other_side = jnp.where(row == index, limits_ref[1, index], other_side)
    first_axis, third_axis = freqs[0:1], freqs[2:3]
    limit = jnp.where(first_axis * third_axis >= 0, same_side, other_side)
    measured = 4 * third_axis * third_axis <= limit * (first_axis * first_axis)
    return jnp.where(measured, 1.0, 0.0).astype(F32)


def chosen_classes(ids_ref, classes):
    ids = ids_ref[...]
    both = jnp.concatenate([ids, ids], axis=1)
    row = lax.broadcasted_iota(jnp.int32, (classes, both.shape[1]), 0)
    return jnp.where(row == both, 1.0, 0.0).astype(F32), both


def mask_rows(spectra, table, chosen):
    measured = jnp.dot(
        table.T.astype(BF16), chosen.astype(BF16), preferred_element_type=F32
    )
    return spectra * measured


def first_mask_kernel(spectra_ref, ids_ref, limits_ref, freqs_ref, out_ref):
    rows = out_ref.shape[0]
    table = wedge_rows(freqs_ref[:, :rows], limits_ref)
    chosen, _ = chosen_classes(ids_ref, limits_ref.shape[1])
    out_ref[...] = mask_rows(spectra_ref[...].astype(F32), table, chosen).astype(BF16)


def split_three(value):
    high = value.astype(BF16).astype(F32)
    rest = value - high
    middle = rest.astype(BF16).astype(F32)
    return high, middle, rest - middle


def rest_mask_kernel(terms, starts, spectra_ref, ids_ref, limits_ref, freqs_ref, done_ref,
                     *out_refs):
    classes = limits_ref.shape[1]
    half = spectra_ref.shape[1] // 2
    chosen, both = chosen_classes(ids_ref, classes)
    spectra = spectra_ref[...].astype(F32)
    power = jnp.zeros((classes, half), F32)
    for index, (rows, start) in enumerate(zip(CUTS, starts)):
        used = min(rows, terms - start)
        table = wedge_rows(chunk_freqs(freqs_ref, start, rows), limits_ref)
        if index == 0:
            masked = done_ref[...].astype(F32)
        else:
            part = spectra[start : start + used]
            if used < rows:
                part = jnp.concatenate([part, jnp.zeros((rows - used, 2 * half), F32)], axis=0)
            masked = mask_rows(part, table, chosen)
        squared = masked * masked
        total = squared + pltpu.roll(squared, half, 1)
        table_part = table.astype(BF16)
        for piece in split_three(total):
            power = power + jnp.dot(
                table_part, piece.astype(BF16), preferred_element_type=F32
            )[:, :half]
        if 0 < index < len(CUTS) - 1:
            out_refs[index - 1][...] = masked.astype(BF16)
    pieces = [jnp.concatenate([piece, piece], axis=1) for piece in split_three(power)]
    ids = jnp.broadcast_to(both.astype(F32), (classes, 2 * half))
    spare = jnp.zeros((rows - used - PAYLOAD, 2 * half), F32)
    masked = jnp.concatenate([masked[:used], *pieces, ids, spare], axis=0)
    out_refs[-1][...] = masked.astype(BF16)


def phase_kernel(starts, freqs_ref, _, *out_refs):
    for rows, start, out_ref in zip(CUTS, starts, out_refs):
        freqs = chunk_freqs(freqs_ref, start, rows).astype(F32)
        turns = jnp.concatenate(
            [a * freqs[0:1] + b * freqs[1:2] + c * freqs[2:3] for a, b, c in SHIFTS]
            + [jnp.zeros((SHIFT_ROWS - COUNT, rows), F32)],
            axis=0,
        )
        angle = turns * (2.0 * math.pi / BOX)
        out_ref[:SHIFT_ROWS] = jnp.cos(angle)
        out_ref[SHIFT_ROWS:] = jnp.sin(angle)


def chunk_kernel(used, first, last, got_ref, sent_ref, core_ref, trig_ref, *refs):
    if first:
        total_ref = None
    else:
        total_ref, *refs = refs
    outs, (high_ref, low_ref, other_ref) = refs[:-3], refs[-3:]
    rows, lanes = got_ref.shape
    half = lanes // 2
    got = got_ref[...].astype(F32)
    sent = sent_ref[...].astype(F32)
    core = core_ref[...].astype(F32)
    other_ref[0:rows, :] = jnp.concatenate([sent[:, :half], core[:, :half]], axis=1).astype(BF16)
    other_ref[rows:, :] = jnp.concatenate([sent[:, half:], core[:, half:]], axis=1).astype(BF16)
    turned = got.T
    if used < rows:
        lane = lax.broadcasted_iota(jnp.int32, (1, rows), 1)
        turned = jnp.where(lane < used, turned, 0.0)
    real, imag = turned[:half], turned[half:]

    def put(row, part, value):
        high = value.astype(BF16)
        high_ref[row : row + half, part * rows : (part + 1) * rows] = high
        low_ref[row : row + half, part * rows : (part + 1) * rows] = (
            value - high.astype(F32)
        ).astype(BF16)

    plain = 2 * COUNT * half
    high_ref[plain:, 0:rows] = real.astype(BF16)
    high_ref[plain:, rows:] = imag.astype(BF16)
    for index in range(COUNT):
        cosine = trig_ref[index : index + 1, :]
        sine = trig_ref[SHIFT_ROWS + index : SHIFT_ROWS + index + 1, :]
        put(index * half, 0, cosine * real)
        put(index * half, 1, cosine * imag)
        put((COUNT + index) * half, 0, sine * imag)
        put((COUNT + index) * half, 1, -sine * real)
    scores_ref = outs[0]
    scores = jnp.dot(high_ref[...], other_ref[...], preferred_element_type=F32)
    if first:
        scores_ref[...] = scores
    else:
        scores_ref[...] = total_ref[...] + scores
    scores_ref[0:plain] += jnp.dot(low_ref[...], other_ref[...], preferred_element_type=F32)
    if not last:
        return

    largest = scores_ref[plain:]
    for index in range(COUNT):
        even = scores_ref[index * half : (index + 1) * half]
        odd = scores_ref[(COUNT + index) * half : (COUNT + index + 1) * half]
        largest = jnp.maximum(largest, even + jnp.abs(odd))
    classes = PAYLOAD // 4
    extra = slice(used, used + PAYLOAD)
    own_extra = got[extra][:, :half]
    other_extra = jnp.concatenate([sent[extra][:, :half], core[extra][:, :half]], axis=1)

    def chosen(ids):
        row = lax.broadcasted_iota(jnp.int32, ids.shape, 0).astype(F32)
        once = jnp.where(row == ids, 1.0, 0.0).astype(F32)
        return jnp.concatenate([once] * 3, axis=0)

    own_chosen = chosen(own_extra[3 * classes :])
    other_chosen = chosen(other_extra[3 * classes :])
    row_norm = jnp.dot(
        own_extra[: 3 * classes].T.astype(BF16),
        other_chosen.astype(BF16),
        preferred_element_type=F32,
    )
    column_norm = jnp.dot(
        own_chosen.T.astype(BF16),
        other_extra[: 3 * classes].astype(BF16),
        preferred_element_type=F32,
    )
    best = largest * lax.rsqrt(row_norm * column_norm + EPSILON)
    outs[1][...] = best
    across = best.T
    outs[2][...] = across[:half]
    outs[3][...] = across[half:]


def chunk_scores(used, first, last, half, got, sent, core, trig, total):
    rows = got.shape[0]
    score_rows = (2 * COUNT + 1) * half
    out_shape = [jax.ShapeDtypeStruct((score_rows, 2 * half), F32)]
    if last:
        out_shape += [
            jax.ShapeDtypeStruct((half, 2 * half), F32),
            jax.ShapeDtypeStruct((half, half), F32),
            jax.ShapeDtypeStruct((half, half), F32),
        ]
    operands = [got, sent, core, trig] + ([] if first else [total])
    return pl.pallas_call(
        lambda *refs: chunk_kernel(used, first, last, *refs),
        out_shape=out_shape,
        in_specs=[VMEM] * len(operands),
        out_specs=[VMEM] * len(out_shape),
        scratch_shapes=[
            pltpu.VMEM((score_rows, 2 * rows), BF16),
            pltpu.VMEM((score_rows - half, 2 * rows), BF16),
            pltpu.VMEM((2 * rows, 2 * half), BF16),
        ],
        compiler_params=pltpu.CompilerParams(vmem_limit_bytes=28 << 20),
        cost_estimate=LOW_COST,
    )(*operands)


def shards(spectra, wedge_ids, tilt_limits, term_freqs):
    terms, lanes = spectra.shape
    half = lanes // 2
    starts = [sum(CUTS[:index]) for index in range(len(CUTS))]
    group, block = lax.axis_index("pair"), lax.axis_index("blk")
    near = near_group(group)
    ids = wedge_ids[None]
    limits = tilt_limits.T

    first_chunk = pl.pallas_call(
        first_mask_kernel,
        grid=(1,),
        out_shape=jax.ShapeDtypeStruct((CUTS[0], lanes), BF16),
        in_specs=[pl.BlockSpec((CUTS[0], lanes), lambda i: (0, 0)), VMEM, SMEM, VMEM],
        out_specs=VMEM,
        cost_estimate=LOW_COST,
    )(spectra, ids, limits, term_freqs)
    rest = pl.pallas_call(
        functools.partial(rest_mask_kernel, terms, starts),
        out_shape=[jax.ShapeDtypeStruct((rows, lanes), BF16) for rows in CUTS[1:]],
        in_specs=[VMEM, VMEM, SMEM, VMEM, VMEM],
        out_specs=[VMEM] * (len(CUTS) - 1),
        cost_estimate=LOW_COST,
    )(spectra, ids, limits, term_freqs, first_chunk)
    kept = [first_chunk, *rest]

    trig = pl.pallas_call(
        functools.partial(phase_kernel, starts),
        out_shape=[jax.ShapeDtypeStruct((2 * SHIFT_ROWS, rows), F32) for rows in CUTS],
        in_specs=[VMEM, ANY],
        out_specs=[VMEM] * len(CUTS),
        cost_estimate=LOW_COST,
    )(term_freqs, kept[-1])
    kept[-1], *trig = lax.optimization_barrier((kept[-1], *trig))
    crossed = [permute(chunk, cross_source) for chunk in kept]
    crossed[0], kept[-1] = lax.optimization_barrier((crossed[0], kept[-1]))

    sent, got, core = [], [], []

    def send(index):
        load = jnp.where(near, kept[index], crossed[index])
        sent.append(load)
        got.append(permute(load, swap_source))
        core.append(permute(load, core_source))

    total = None
    last = len(CUTS) - 1
    for index in range(last):
        send(index)
    for index, start in enumerate(starts):
        used = min(CUTS[index], terms - start)
        total, *tiles = chunk_scores(
            used, index == 0, index == last, half, got[index], sent[index], core[index],
            trig[index], total,
        )
        if index == 0:
            crossed[last], total = lax.optimization_barrier((crossed[last], total))
            send(last)
    rows_tile, own_tile, core_tile = tiles
    rows_back = permute(rows_tile, first_back_source)
    own_back = permute(own_tile, own_back_source)
    core_back = permute(core_tile, second_back_source)

    single = jnp.where(near, own_tile, own_back)
    own_part, core_part = rows_back[:, :half], rows_back[:, half:]
    even = block % 2 == 0
    lead = near == even
    return jnp.concatenate(
        [
            jnp.where(lead, core_part, core_back),
            jnp.where(even, single, own_part),
            jnp.where(lead, core_back, core_part),
            jnp.where(even, own_part, single),
        ],
        axis=1,
    )


def solution(mesh):
    placed = (P(None, AXES), P(AXES), P(), P())
    return jax.shard_map(
        shards, mesh=mesh, in_specs=placed, out_specs=P(AXES, None), check_vma=False
    )
```

```python
import functools
import math

import jax
import jax.numpy as jnp
from jax import lax
from jax.experimental import pallas as pl
from jax.experimental.pallas import tpu as pltpu
from jax.sharding import PartitionSpec as P

BOX = 24
RADIUS = 1
ROUND = 2
EPSILON = 1e-06
PAYLOAD = 32
LANES = 128
CUTS = (1024, 1024, 1024)
AXES = ("pair", "blk")
F32 = jnp.float32
BF16 = jnp.bfloat16

SHIFTS = tuple(
    (a, b, c)
    for a in range(-RADIUS, RADIUS + 1)
    for b in range(-RADIUS, RADIUS + 1)
    for c in range(-RADIUS, RADIUS + 1)
    if (a, b, c) > (0, 0, 0)
)
COUNT = len(SHIFTS)
SHIFT_ROWS = 16
VMEM = pl.BlockSpec(memory_space=pltpu.VMEM)
SMEM = pl.BlockSpec(memory_space=pltpu.SMEM)
ANY = pl.BlockSpec(memory_space=pl.ANY)
LOW_COST = pl.CostEstimate(flops=1, bytes_accessed=1, transcendentals=0)


def near_group(group):
    return (group >> 1 ^ group) & 1 == 0


def permute(value, route):
    pairs_n, blocks_n = lax.axis_size("pair"), lax.axis_size("blk")
    table = []
    for group in range(pairs_n):
        for block in range(blocks_n):
            place = route(group, block, blocks_n)
            if place is not None:
                source = place[0] * blocks_n + place[1] % blocks_n
                table.append((source, group * blocks_n + block))
    return lax.ppermute(value, AXES, table)


def cross_source(group, block, count):
    if near_group(group):
        return None
    return group ^ 1 ^ ROUND, block - 2 if block % 2 == 0 else block


def swap_source(group, block, count):
    if near_group(group):
        return group ^ 1, block + 4 if block % 2 == 0 else block - 2
    return group ^ 1, block if block % 2 == 0 else block - 2


def core_source(group, block, count):
    return group, block ^ 1


def own_back_source(group, block, count):
    if near_group(group):
        return None
    return group ^ 1 ^ ROUND, block + 2 if block % 2 == 0 else block


def first_back_source(group, block, count):
    if near_group(group):
        return group ^ 1, block if block % 2 == 0 else block + 2
    return group ^ ROUND, block - 2 if block % 2 == 0 else block + 2


def chunk_freqs(freqs_ref, start, rows):
    axes, terms = freqs_ref.shape
    if start + rows <= terms:
        return freqs_ref[:, start : start + rows]
    spare = jnp.zeros((axes, start + rows - terms), jnp.int32)
    return jnp.concatenate([freqs_ref[:, start:], spare], axis=1)


def wedge_rows(freqs, limits_ref):
    classes = limits_ref.shape[1]
    row = lax.broadcasted_iota(jnp.int32, (classes, 1), 0)
    same_side = jnp.zeros((classes, 1), jnp.int32)
    other_side = jnp.zeros((classes, 1), jnp.int32)
    for index in range(classes):
        same_side = jnp.where(row == index, limits_ref[0, index], same_side)
        other_side = jnp.where(row == index, limits_ref[1, index], other_side)
    first_axis, third_axis = freqs[0:1], freqs[2:3]
    limit = jnp.where(first_axis * third_axis >= 0, same_side, other_side)
    measured = 4 * third_axis * third_axis <= limit * (first_axis * first_axis)
    return jnp.where(measured, 1.0, 0.0).astype(F32)


def chosen_classes(ids_ref, classes):
    ids = ids_ref[...]
    both = jnp.concatenate([ids, ids], axis=1)
    row = lax.broadcasted_iota(jnp.int32, (classes, both.shape[1]), 0)
    return jnp.where(row == both, 1.0, 0.0).astype(F32), both


def mask_rows(spectra, table, chosen):
    measured = jnp.dot(
        table.T.astype(BF16), chosen.astype(BF16), preferred_element_type=F32
    )
    return spectra * measured


def first_mask_kernel(spectra_ref, ids_ref, limits_ref, freqs_ref, out_ref):
    rows = out_ref.shape[0]
    table = wedge_rows(freqs_ref[:, :rows], limits_ref)
    chosen, _ = chosen_classes(ids_ref, limits_ref.shape[1])
    out_ref[...] = mask_rows(spectra_ref[...].astype(F32), table, chosen).astype(BF16)


def split_three(value):
    high = value.astype(BF16).astype(F32)
    rest = value - high
    middle = rest.astype(BF16).astype(F32)
    return high, middle, rest - middle


def rest_mask_kernel(terms, starts, spectra_ref, ids_ref, limits_ref, freqs_ref, done_ref,
                     *out_refs):
    classes = limits_ref.shape[1]
    half = spectra_ref.shape[1] // 2
    chosen, both = chosen_classes(ids_ref, classes)
    spectra = spectra_ref[...].astype(F32)
    power = jnp.zeros((classes, half), F32)
    for index, (rows, start) in enumerate(zip(CUTS, starts)):
        used = min(rows, terms - start)
        table = wedge_rows(chunk_freqs(freqs_ref, start, rows), limits_ref)
        if index == 0:
            masked = done_ref[...].astype(F32)
        else:
            part = spectra[start : start + used]
            if used < rows:
                part = jnp.concatenate([part, jnp.zeros((rows - used, 2 * half), F32)], axis=0)
            masked = mask_rows(part, table, chosen)
        squared = masked * masked
        total = squared + pltpu.roll(squared, half, 1)
        table_part = table.astype(BF16)
        for piece in split_three(total):
            power = power + jnp.dot(
                table_part, piece.astype(BF16), preferred_element_type=F32
            )[:, :half]
        if 0 < index < len(CUTS) - 1:
            out_refs[index - 1][...] = masked.astype(BF16)
    pieces = [jnp.concatenate([piece, piece], axis=1) for piece in split_three(power)]
    ids = jnp.broadcast_to(both.astype(F32), (classes, 2 * half))
    spare = jnp.zeros((rows - used - PAYLOAD, 2 * half), F32)
    masked = jnp.concatenate([masked[:used], *pieces, ids, spare], axis=0)
    out_refs[-1][...] = masked.astype(BF16)


def phase_kernel(starts, freqs_ref, _, *out_refs):
    for rows, start, out_ref in zip(CUTS, starts, out_refs):
        freqs = chunk_freqs(freqs_ref, start, rows).astype(F32)
        turns = jnp.concatenate(
            [a * freqs[0:1] + b * freqs[1:2] + c * freqs[2:3] for a, b, c in SHIFTS]
            + [jnp.zeros((SHIFT_ROWS - COUNT, rows), F32)],
            axis=0,
        )
        angle = turns * (2.0 * math.pi / BOX)
        out_ref[:SHIFT_ROWS] = jnp.cos(angle)
        out_ref[SHIFT_ROWS:] = jnp.sin(angle)


def chunk_kernel(used, first, last, got_ref, sent_ref, core_ref, trig_ref, *refs):
    if first:
        total_ref = None
    else:
        total_ref, *refs = refs
    outs, (high_ref, low_ref, other_ref) = refs[:-3], refs[-3:]
    rows, lanes = got_ref.shape
    half = lanes // 2
    got = got_ref[...].astype(F32)
    sent = sent_ref[...].astype(F32)
    core = core_ref[...].astype(F32)
    other_ref[0:rows, :] = jnp.concatenate([sent[:, :half], core[:, :half]], axis=1).astype(BF16)
    other_ref[rows:, :] = jnp.concatenate([sent[:, half:], core[:, half:]], axis=1).astype(BF16)
    turned = got.T
    if used < rows:
        lane = lax.broadcasted_iota(jnp.int32, (1, rows), 1)
        turned = jnp.where(lane < used, turned, 0.0)
    real, imag = turned[:half], turned[half:]

    def put(row, part, value):
        high = value.astype(BF16)
        high_ref[row : row + half, part * rows : (part + 1) * rows] = high
        low_ref[row : row + half, part * rows : (part + 1) * rows] = (
            value - high.astype(F32)
        ).astype(BF16)

    plain = 2 * COUNT * half
    high_ref[plain:, 0:rows] = real.astype(BF16)
    high_ref[plain:, rows:] = imag.astype(BF16)
    for index in range(COUNT):
        cosine = trig_ref[index : index + 1, :]
        sine = trig_ref[SHIFT_ROWS + index : SHIFT_ROWS + index + 1, :]
        put(index * half, 0, cosine * real)
        put(index * half, 1, cosine * imag)
        put((COUNT + index) * half, 0, sine * imag)
        put((COUNT + index) * half, 1, -sine * real)
    scores_ref = outs[0]
    scores = jnp.dot(high_ref[...], other_ref[...], preferred_element_type=F32)
    if first:
        scores_ref[...] = scores
    else:
        scores_ref[...] = total_ref[...] + scores
    scores_ref[0:plain] += jnp.dot(low_ref[...], other_ref[...], preferred_element_type=F32)
    if not last:
        return

    largest = scores_ref[plain:]
    for index in range(COUNT):
        even = scores_ref[index * half : (index + 1) * half]
        odd = scores_ref[(COUNT + index) * half : (COUNT + index + 1) * half]
        largest = jnp.maximum(largest, even + jnp.abs(odd))
    classes = PAYLOAD // 4
    extra = slice(used, used + PAYLOAD)
    own_extra = got[extra][:, :half]
    other_extra = jnp.concatenate([sent[extra][:, :half], core[extra][:, :half]], axis=1)

    def chosen(ids):
        row = lax.broadcasted_iota(jnp.int32, ids.shape, 0).astype(F32)
        once = jnp.where(row == ids, 1.0, 0.0).astype(F32)
        return jnp.concatenate([once] * 3, axis=0)

    own_chosen = chosen(own_extra[3 * classes :])
    other_chosen = chosen(other_extra[3 * classes :])
    row_norm = jnp.dot(
        own_extra[: 3 * classes].T.astype(BF16),
        other_chosen.astype(BF16),
        preferred_element_type=F32,
    )
    column_norm = jnp.dot(
        own_chosen.T.astype(BF16),
        other_extra[: 3 * classes].astype(BF16),
        preferred_element_type=F32,
    )
    best = largest * lax.rsqrt(row_norm * column_norm + EPSILON)
    outs[1][...] = best
    across = best.T
    outs[2][...] = across[:half]
    outs[3][...] = across[half:]


def chunk_scores(used, first, last, half, got, sent, core, trig, total):
    rows = got.shape[0]
    score_rows = (2 * COUNT + 1) * half
    out_shape = [jax.ShapeDtypeStruct((score_rows, 2 * half), F32)]
    if last:
        out_shape += [
            jax.ShapeDtypeStruct((half, 2 * half), F32),
            jax.ShapeDtypeStruct((half, half), F32),
            jax.ShapeDtypeStruct((half, half), F32),
        ]
    operands = [got, sent, core, trig] + ([] if first else [total])
    return pl.pallas_call(
        lambda *refs: chunk_kernel(used, first, last, *refs),
        out_shape=out_shape,
        in_specs=[VMEM] * len(operands),
        out_specs=[VMEM] * len(out_shape),
        scratch_shapes=[
            pltpu.VMEM((score_rows, 2 * rows), BF16),
            pltpu.VMEM((score_rows - half, 2 * rows), BF16),
            pltpu.VMEM((2 * rows, 2 * half), BF16),
        ],
        compiler_params=pltpu.CompilerParams(vmem_limit_bytes=28 << 20),
        cost_estimate=LOW_COST,
    )(*operands)


def shards(spectra, wedge_ids, tilt_limits, term_freqs):
    terms, lanes = spectra.shape
    half = lanes // 2
    starts = [sum(CUTS[:index]) for index in range(len(CUTS))]
    group, block = lax.axis_index("pair"), lax.axis_index("blk")
    near = near_group(group)
    ids = wedge_ids[None]
    limits = tilt_limits.T

    first_chunk = pl.pallas_call(
        first_mask_kernel,
        grid=(1,),
        out_shape=jax.ShapeDtypeStruct((CUTS[0], lanes), BF16),
        in_specs=[pl.BlockSpec((CUTS[0], lanes), lambda i: (0, 0)), VMEM, SMEM, VMEM],
        out_specs=VMEM,
        cost_estimate=LOW_COST,
    )(spectra, ids, limits, term_freqs)
    rest = pl.pallas_call(
        functools.partial(rest_mask_kernel, terms, starts),
        out_shape=[jax.ShapeDtypeStruct((rows, lanes), BF16) for rows in CUTS[1:]],
        in_specs=[VMEM, VMEM, SMEM, VMEM, VMEM],
        out_specs=[VMEM] * (len(CUTS) - 1),
        cost_estimate=LOW_COST,
    )(spectra, ids, limits, term_freqs, first_chunk)
    kept = [first_chunk, *rest]

    crossed = [permute(chunk, cross_source) for chunk in kept]
    crossed[0], kept[-1] = lax.optimization_barrier((crossed[0], kept[-1]))
    trig = pl.pallas_call(
        functools.partial(phase_kernel, starts),
        out_shape=[jax.ShapeDtypeStruct((2 * SHIFT_ROWS, rows), F32) for rows in CUTS],
        in_specs=[VMEM, ANY],
        out_specs=[VMEM] * len(CUTS),
        cost_estimate=LOW_COST,
    )(term_freqs, crossed[0])

    sent, got, core = [], [], []

    def send(index):
        load = jnp.where(near, kept[index], crossed[index])
        sent.append(load)
        got.append(permute(load, swap_source))
        core.append(permute(load, core_source))

    total = None
    last = len(CUTS) - 1
    for index in range(last):
        send(index)
    for index, start in enumerate(starts):
        used = min(CUTS[index], terms - start)
        total, *tiles = chunk_scores(
            used, index == 0, index == last, half, got[index], sent[index], core[index],
            trig[index], total,
        )
        if index == 0:
            crossed[last], total = lax.optimization_barrier((crossed[last], total))
            send(last)
    rows_tile, own_tile, core_tile = tiles
    rows_back = permute(rows_tile, first_back_source)
    core_back = permute(core_tile, core_source)
    both_back = permute(jnp.concatenate([own_tile, core_back], axis=1), own_back_source)

    single = jnp.where(near, own_tile, both_back[:, :half])
    core_back = jnp.where(near, core_back, both_back[:, half:])
    own_part, core_part = rows_back[:, :half], rows_back[:, half:]
    even = block % 2 == 0
    lead = near == even
    return jnp.concatenate(
        [
            jnp.where(lead, core_part, core_back),
            jnp.where(even, single, own_part),
            jnp.where(lead, core_back, core_part),
            jnp.where(even, own_part, single),
        ],
        axis=1,
    )


def solution(mesh):
    placed = (P(None, AXES), P(AXES), P(), P())
    return jax.shard_map(
        shards, mesh=mesh, in_specs=placed, out_specs=P(AXES, None), check_vma=False
    )
```
